32 devices in a mesh: clip: 8 (over y, x, core), frame: 4 (over z).
Axes of the slice: x: 2, y: 2, z: 4, core: 2. Of those that a mesh axis runs over, the one named last changes fastest.
Arguments:
- layer_input: bfloat16 [4096, 768], P(('clip', 'frame')), may hold values from -6 to 6
- first_gain: bfloat16 [768], P(('clip', 'frame')), may hold values from 0.5 to 1.5
- first_bias: bfloat16 [768], P(('clip', 'frame')), may hold values from -3 to 3
- query_weight: bfloat16 [768, 768], P(('clip', 'frame')), may hold values from -0.21875 to 0.21875
- query_bias: bfloat16 [768], P(('clip', 'frame')), may hold values from -3 to 3
- key_weight: bfloat16 [768, 768], P(('clip', 'frame')), may hold values from -0.21875 to 0.21875
- value_weight: bfloat16 [768, 768], P(('clip', 'frame')), may hold values from -0.21875 to 0.21875
- value_bias: bfloat16 [768], P(('clip', 'frame')), may hold values from -3 to 3
- output_weight: bfloat16 [768, 768], P(('clip', 'frame')), may hold values from -1.75 to 1.75
- output_bias: bfloat16 [768], P(('clip', 'frame')), may hold values from -3 to 3
- second_gain: bfloat16 [768], P(('clip', 'frame')), may hold values from 0.5 to 1.5
- second_bias: bfloat16 [768], P(('clip', 'frame')), may hold values from -3 to 3
- inner_weight: bfloat16 [768, 3072], P(('clip', 'frame')), may hold values from -0.21875 to 0.21875
- inner_bias: bfloat16 [3072], P(('clip', 'frame')), may hold values from -3 to 3
- outer_weight: bfloat16 [3072, 768], P(('clip', 'frame')), may hold values from -0.15625 to 0.15625
- outer_bias: bfloat16 [768], P(('clip', 'frame')), may hold values from -3 to 3
- upstream: bfloat16 [4096, 768], P(('clip', 'frame')), may hold values from -6 to 6
Outputs:
- layer_output: bfloat16 [4096, 768], P(('clip', 'frame'))
- input_grad: bfloat16 [4096, 768], P(('clip', 'frame'))
- grad_first_gain: float32 [768], P(('clip', 'frame'))
- grad_first_bias: float32 [768], P(('clip', 'frame'))
- grad_query_weight: float32 [768, 768], P(('clip', 'frame'))
- grad_query_bias: float32 [768], P(('clip', 'frame'))
- grad_key_weight: float32 [768, 768], P(('clip', 'frame'))
- grad_value_weight: float32 [768, 768], P(('clip', 'frame'))
- grad_value_bias: float32 [768], P(('clip', 'frame'))
- grad_output_weight: float32 [768, 768], P(('clip', 'frame'))
- grad_output_bias: float32 [768], P(('clip', 'frame'))
- grad_second_gain: float32 [768], P(('clip', 'frame'))
- grad_second_bias: float32 [768], P(('clip', 'frame'))
- grad_inner_weight: float32 [768, 3072], P(('clip', 'frame'))
- grad_inner_bias: float32 [3072], P(('clip', 'frame'))
- grad_outer_weight: float32 [3072, 768], P(('clip', 'frame'))
- grad_outer_bias: float32 [768], P(('clip', 'frame'))
The draws below stay inside these ranges and needn't reach their ends.
All inputs are finite; a program needn't handle non-finite values.
Results may differ from the reference program's by a relative error of at most 0.012.
The reference program's roundings to bfloat16 on the way count: a program that leaves them out, or rounds other values in their place, can miss the bound.
Values may be sent and summed in bfloat16 or wider, within the bound.
A program may use at most 192 MiB of HBM per device.

```python
import jax
import jax.numpy as jnp
from jax import lax

D = 768
HEADS = 12
HEAD_DIM = 64
FF = 3072
LENGTH = 512
CLIPS = 8
TOKENS = 4096


def raised(entries, stream_key, source, target, parts, factor):
    def block_of(position):
        return (jnp.arange(entries.shape[position]) // (entries.shape[position] // parts)).reshape((-1,) + (1,) * (entries.ndim - 1 - position))

    one_side = jax.random.permutation(stream_key, parts)[block_of(target)]
    other_side = (block_of(target) + parts // 2) % parts
    return jnp.where((block_of(source) == one_side) | (block_of(source) == other_side), factor * entries, entries)


def block_levels(own_key, shape, cuts, smallest, high):
    gain, own = 1.0, jax.random.fold_in(own_key, 6)
    for axis_at, shards_of in cuts:
        draws = jnp.exp(jax.random.uniform(jax.random.fold_in(own, axis_at), (shards_of,), jnp.float32, smallest / len(cuts), high / len(cuts)))
        gain = gain * jnp.repeat(draws, shape[axis_at] // shards_of).reshape([-1 if axis == axis_at else 1 for axis in range(len(shape))])
    return gain


def scatter_about(own_key, dims, scale, reach, shards=(), dtype=jnp.bfloat16):
    level = block_levels(own_key, dims, shards, -0.22, 0.18) if shards else 1.0
    values = jax.random.normal(own_key, dims, jnp.float32) * scale * level
    return jnp.minimum(jnp.maximum(values, -reach), reach).astype(dtype)


def bell_draw_with(stream_key, dims, width, bound, shards, heavy, dtype=jnp.bfloat16):
    drawn = width * jax.random.normal(stream_key, dims, jnp.float32)
    if shards:
        drawn = drawn * block_levels(stream_key, dims, shards, -0.22, 0.18)
    return jnp.clip(raised(drawn, jax.random.fold_in(stream_key, 3), *heavy), -bound, bound).astype(dtype)


def setup_inputs(seed: int = 0) -> dict:
    arg_keys = jax.random.split(jax.random.key(seed), 18)
    layer_input = scatter_about(arg_keys[0], (TOKENS, D), 1.0, 6.0, ((0, 32),))
    first_gain = jnp.clip(1.0 + 0.1 * jax.random.normal(arg_keys[1], (D,), jnp.float32), 0.5, 1.5).astype(jnp.bfloat16)
    first_bias = scatter_about(arg_keys[2], (D,), 0.5, 3.0, ((0, 32),))
    query_weight = scatter_about(arg_keys[3], (D, D), D ** -0.5, 0.21875, ((0, 32),))
    query_bias = scatter_about(arg_keys[4], (D,), 0.5, 3.0, ((0, 32),))
    key_weight = scatter_about(arg_keys[5], (D, D), D ** -0.5, 0.21875, ((0, 32),))
    value_weight = scatter_about(arg_keys[6], (D, D), D ** -0.5, 0.21875, ((0, 32),))
    value_bias = scatter_about(arg_keys[7], (D,), 0.5, 3.0, ((0, 32),))
    output_weight = scatter_about(arg_keys[8], (D, D), (D // 64) ** -0.5, 1.75, ((0, 32),))
    output_bias = scatter_about(arg_keys[9], (D,), 0.5, 3.0, ((0, 32),))
    second_gain = jnp.clip(1.0 + 0.1 * jax.random.normal(arg_keys[10], (D,), jnp.float32), 0.5, 1.5).astype(jnp.bfloat16)
    second_bias = scatter_about(arg_keys[11], (D,), 0.5, 3.0, ((0, 32),))
    inner_weight = scatter_about(arg_keys[12], (D, FF), D ** -0.5, 0.21875, ((0, 32),))
    inner_bias = scatter_about(arg_keys[13], (FF,), 0.5, 3.0, ((0, 32),))
    outer_weight = scatter_about(arg_keys[14], (FF, D), (FF // 2) ** -0.5, 0.15625, ((0, 32),))
    outer_bias = scatter_about(arg_keys[15], (D,), 0.5, 3.0, ((0, 32),))
    upstream = bell_draw_with(arg_keys[16], (TOKENS, D), 1.0, 6.0, ((0, 32),), (0, 1, 32, 2.75))
    return {"layer_input": layer_input, "first_gain": first_gain, "first_bias": first_bias, "query_weight": query_weight, "query_bias": query_bias, "key_weight": key_weight, "value_weight": value_weight, "value_bias": value_bias, "output_weight": output_weight, "output_bias": output_bias, "second_gain": second_gain, "second_bias": second_bias, "inner_weight": inner_weight, "inner_bias": inner_bias, "outer_weight": outer_weight, "outer_bias": outer_bias, "upstream": upstream}


EPS = 1e-05
SQRT_HALF = 0.7071067811865476
INV_ROOT = 0.3989422804014327

def normalize(rows):
    mean = lax.optimization_barrier(jnp.mean(rows, axis=-1, keepdims=True))
    centered = rows - mean
    rstd = lax.rsqrt(lax.optimization_barrier(jnp.mean(centered * centered, axis=-1, keepdims=True)) + EPS)
    return (centered * rstd, rstd)

def norm_back(grad_norm, normed, rstd):
    first = lax.optimization_barrier(jnp.mean(grad_norm, axis=-1, keepdims=True))
    second = lax.optimization_barrier(jnp.mean(grad_norm * normed, axis=-1, keepdims=True))
    return rstd * (grad_norm - first - normed * second)

def gelu_slope(inner):
    return 0.5 * (1.0 + lax.erf(inner * SQRT_HALF)) + inner * jnp.exp(-0.5 * inner * inner) * INV_ROOT

def matmul(left, right):
    return jnp.dot(left, right, preferred_element_type=jnp.float32)

def clip_pass(params, clip_input, clip_upstream):
    pre_gain, pre_shift, query_mat, query_add, key_mat, value_mat, value_add, proj_mat, proj_add, post_gain, post_shift, inner_mat, inner_add, outer_mat, outer_add = params
    f32 = jnp.float32
    bf16 = jnp.bfloat16
    scale = HEAD_DIM ** (-0.5)
    rows = clip_input.astype(f32)
    first_norm, first_rstd = normalize(rows)
    first_hidden = (first_norm * pre_gain.astype(f32) + pre_shift.astype(f32)).astype(bf16)
    queries = ((matmul(first_hidden, query_mat) + query_add.astype(f32)) * scale).astype(bf16)
    keys = matmul(first_hidden, key_mat).astype(bf16)
    values = (matmul(first_hidden, value_mat) + value_add.astype(f32)).astype(bf16)
    q_heads = queries.reshape(LENGTH, HEADS, HEAD_DIM).astype(f32)
    k_heads = keys.reshape(LENGTH, HEADS, HEAD_DIM).astype(f32)
    v_heads = values.reshape(LENGTH, HEADS, HEAD_DIM).astype(f32)
    scores = jnp.einsum('qhd,khd->hqk', q_heads, k_heads)
    log_total = jax.nn.logsumexp(scores, axis=-1, keepdims=True)
    chance = jnp.exp(scores - log_total)
    probs = chance.astype(bf16)
    attended = jnp.einsum('hqk,khd->qhd', probs.astype(f32), v_heads).reshape(LENGTH, D).astype(bf16)
    middle = rows + matmul(attended, proj_mat) + proj_add.astype(f32)
    second_norm, second_rstd = normalize(middle)
    second_hidden = (second_norm * post_gain.astype(f32) + post_shift.astype(f32)).astype(bf16)
    inner = matmul(second_hidden, inner_mat) + inner_add.astype(f32)
    activated = jax.nn.gelu(inner, approximate=False).astype(bf16)
    layer_output = (middle + matmul(activated, outer_mat) + outer_add.astype(f32)).astype(bf16)
    grad_out = clip_upstream.astype(f32)
    g_outer_w = matmul(activated.T, clip_upstream)
    g_outer_b = lax.optimization_barrier(jnp.sum(grad_out, axis=0))
    grad_inner = matmul(clip_upstream, outer_mat.T) * gelu_slope(inner)
    inner_round = grad_inner.astype(bf16)
    g_inner_w = matmul(second_hidden.T, inner_round)
    g_inner_b = lax.optimization_barrier(jnp.sum(grad_inner, axis=0))
    grad_second = matmul(inner_round, inner_mat.T)
    g_second_g = lax.optimization_barrier(jnp.sum(grad_second * second_norm, axis=0))
    g_second_b = lax.optimization_barrier(jnp.sum(grad_second, axis=0))
    grad_middle = grad_out + norm_back(grad_second * post_gain.astype(f32), second_norm, second_rstd)
    middle_round = grad_middle.astype(bf16)
    g_proj_w = matmul(attended.T, middle_round)
    g_proj_b = lax.optimization_barrier(jnp.sum(grad_middle, axis=0))
    grad_attended = matmul(middle_round, proj_mat.T).astype(bf16)
    g_heads = grad_attended.reshape(LENGTH, HEADS, HEAD_DIM).astype(f32)
    a_heads = attended.reshape(LENGTH, HEADS, HEAD_DIM).astype(f32)
    grad_probs = jnp.einsum('qhd,khd->hqk', g_heads, v_heads)
    offsets = jnp.einsum('qhd,qhd->hq', g_heads, a_heads)[:, :, None]
    grad_scores = (chance * (grad_probs - offsets)).astype(bf16).astype(f32)
    grad_queries = (jnp.einsum('hqk,khd->qhd', grad_scores, k_heads) * scale).reshape(LENGTH, D)
    grad_keys = jnp.einsum('hqk,qhd->khd', grad_scores, q_heads).reshape(LENGTH, D)
    grad_values = jnp.einsum('hqk,qhd->khd', probs.astype(f32), g_heads).reshape(LENGTH, D)
    query_round = grad_queries.astype(bf16)
    key_round = grad_keys.astype(bf16)
    value_round = grad_values.astype(bf16)
    g_query_w = matmul(first_hidden.T, query_round)
    g_key_w = matmul(first_hidden.T, key_round)
    g_value_w = matmul(first_hidden.T, value_round)
    g_query_b = lax.optimization_barrier(jnp.sum(grad_queries, axis=0))
    g_value_b = lax.optimization_barrier(jnp.sum(grad_values, axis=0))
    grad_first = matmul(query_round, query_mat.T) + matmul(key_round, key_mat.T) + matmul(value_round, value_mat.T)
    g_first_g = lax.optimization_barrier(jnp.sum(grad_first * first_norm, axis=0))
    g_first_b = lax.optimization_barrier(jnp.sum(grad_first, axis=0))
    input_grad = (grad_middle + norm_back(grad_first * pre_gain.astype(f32), first_norm, first_rstd)).astype(bf16)
    grads = (g_first_g, g_first_b, g_query_w, g_query_b, g_key_w, g_value_w, g_value_b, g_proj_w, g_proj_b, g_second_g, g_second_b, g_inner_w, g_inner_b, g_outer_w, g_outer_b)
    return (layer_output, input_grad, grads)

def reference(layer_input, first_gain, first_bias, query_weight, query_bias, key_weight, value_weight, value_bias, output_weight, output_bias, second_gain, second_bias, inner_weight, inner_bias, outer_weight, outer_bias, upstream):
    params = (first_gain, first_bias, query_weight, query_bias, key_weight, value_weight, value_bias, output_weight, output_bias, second_gain, second_bias, inner_weight, inner_bias, outer_weight, outer_bias)
    clip_inputs = layer_input.reshape(CLIPS, LENGTH, D)
    clip_ups = upstream.reshape(CLIPS, LENGTH, D)
    zeros = tuple((jnp.zeros(item.shape, jnp.float32) for item in params))

    def advance(carry, pair):
        produced, backward, grads = clip_pass(params, pair[0], pair[1])
        return (tuple((left + right for left, right in zip(carry, grads))), (produced, backward))
    totals, (produced, backward) = lax.scan(advance, zeros, (clip_inputs, clip_ups))
    return (produced.reshape(TOKENS, D), backward.reshape(TOKENS, D), totals[0], totals[1], totals[2], totals[3], totals[4], totals[5], totals[6], totals[7], totals[8], totals[9], totals[10], totals[11], totals[12], totals[13], totals[14])
```

```python
import jax
import jax.numpy as jnp
from jax import lax
from jax.sharding import PartitionSpec as P

HEADS = 12
HEAD_DIM = 64


EPS = 1e-05
SQRT_HALF = 0.7071067811865476
INV_ROOT = 0.3989422804014327


def normalize(rows):
    mean = jnp.mean(rows, axis=-1, keepdims=True)
    centered = rows - mean
    rstd = lax.rsqrt(jnp.mean(centered * centered, axis=-1, keepdims=True) + EPS)
    return (centered * rstd, rstd)


def norm_back(grad_norm, normed, rstd):
    first = jnp.mean(grad_norm, axis=-1, keepdims=True)
    second = jnp.mean(grad_norm * normed, axis=-1, keepdims=True)
    return rstd * (grad_norm - first - normed * second)


def gelu_slope(inner):
    return (
        0.5 * (1.0 + lax.erf(inner * SQRT_HALF)) + inner * jnp.exp(-0.5 * inner * inner) * INV_ROOT
    )


def matmul(left, right):
    return jnp.dot(left, right, preferred_element_type=jnp.float32)


def left_product(left, right):
    return jnp.einsum("ti,to->io", left, right, preferred_element_type=jnp.float32)


def right_product(left, right):
    return jnp.einsum("to,io->ti", left, right, preferred_element_type=jnp.float32)


AXES = ("clip", "frame")
f32 = jnp.float32
bf16 = jnp.bfloat16


def as_columns(vectors, rows):
    return jnp.concatenate([item.reshape(-1, rows).T for item in vectors], axis=1)


def gather_rows(part):
    return lax.all_gather(part, AXES, axis=0, tiled=True)


def scatter_rows(part):
    half = lax.psum_scatter(part, "clip", scatter_dimension=0, tiled=True)
    return lax.psum_scatter(half, "frame", scatter_dimension=0, tiled=True)


def body(
    layer_input,
    first_gain,
    first_bias,
    query_weight,
    query_bias,
    key_weight,
    value_weight,
    value_bias,
    output_weight,
    output_bias,
    second_gain,
    second_bias,
    inner_weight,
    inner_bias,
    outer_weight,
    outer_bias,
    upstream,
):
    scale = HEAD_DIM ** (-0.5)
    own = query_weight.shape[0]
    vectors = (
        first_gain,
        first_bias,
        query_bias,
        value_bias,
        output_bias,
        second_gain,
        second_bias,
        outer_bias,
    )
    small = as_columns(vectors + (inner_bias,), own)
    spare = -small.shape[1] % 128
    small = jnp.pad(small, ((0, 0), (0, spare)))
    sizes = (
        query_weight.shape[1],
        key_weight.shape[1],
        value_weight.shape[1],
        output_weight.shape[1],
        inner_weight.shape[1],
        small.shape[1],
    )
    ends = []
    for size in sizes:
        ends.append((ends[-1] if ends else 0) + size)
    wide = gather_rows(
        jnp.concatenate(
            [query_weight, key_weight, value_weight, output_weight, inner_weight, small], axis=1
        )
    )
    wide, outer_weight = lax.optimization_barrier((wide, outer_weight))
    outer_mat = gather_rows(outer_weight)
    (query_mat, key_mat, value_mat, proj_mat, inner_mat, shared) = jnp.split(wide, ends[:-1], axis=1)
    total = query_mat.shape[0]
    (pre_gain, pre_shift, query_add, value_add, proj_add, post_gain, post_shift, outer_add) = [
        shared[:, at] for at in range(8)
    ]
    per = inner_bias.shape[0] // own
    inner_add = (
        shared[:, 8 : 8 + per].reshape(total // own, own, per).transpose(0, 2, 1).reshape(-1)
    )
    local = layer_input.shape[0]
    width = layer_input.shape[1]
    rows = layer_input.astype(f32)
    first_norm, first_rstd = normalize(rows)
    first_hidden = (first_norm * pre_gain.astype(f32) + pre_shift.astype(f32)).astype(bf16)
    queries = ((matmul(first_hidden, query_mat) + query_add.astype(f32)) * scale).astype(bf16)
    keys = matmul(first_hidden, key_mat).astype(bf16)
    values = (matmul(first_hidden, value_mat) + value_add.astype(f32)).astype(bf16)
    both = lax.all_gather(jnp.concatenate([keys, values], axis=1), "frame", axis=0, tiled=True)
    all_keys, all_values = both[:, :width], both[:, width:]
    q_heads = queries.reshape(local, HEADS, HEAD_DIM)
    k_heads = all_keys.reshape(-1, HEADS, HEAD_DIM)
    v_heads = all_values.reshape(-1, HEADS, HEAD_DIM)
    scores = jnp.einsum("qhd,khd->hqk", q_heads, k_heads, preferred_element_type=f32)
    log_total = jax.nn.logsumexp(scores, axis=-1, keepdims=True)
    probs = jnp.exp(scores - log_total).astype(bf16)
    attended = (
        jnp.einsum("hqk,khd->qhd", probs, v_heads, preferred_element_type=f32)
        .reshape(local, width)
        .astype(bf16)
    )
    middle = rows + matmul(attended, proj_mat) + proj_add.astype(f32)
    second_norm, second_rstd = normalize(middle)
    second_hidden = (second_norm * post_gain.astype(f32) + post_shift.astype(f32)).astype(bf16)
    inner = matmul(second_hidden, inner_mat) + inner_add.astype(f32)
    activated = jax.nn.gelu(inner, approximate=False).astype(bf16)
    layer_output = (middle + matmul(activated, outer_mat) + outer_add.astype(f32)).astype(bf16)
    grad_out = upstream.astype(f32)
    g_outer_w = left_product(activated, upstream)
    g_outer_b = jnp.sum(grad_out, axis=0)
    grad_inner = right_product(upstream, outer_mat) * gelu_slope(inner)
    inner_round = grad_inner.astype(bf16)
    g_inner_w = left_product(second_hidden, inner_round)
    g_inner_b = jnp.sum(grad_inner, axis=0)
    grad_second = right_product(inner_round, inner_mat)
    g_second_g = jnp.sum(grad_second * second_norm, axis=0)
    g_second_b = jnp.sum(grad_second, axis=0)
    grad_middle = grad_out + norm_back(
        grad_second * post_gain.astype(f32), second_norm, second_rstd
    )
    middle_round = grad_middle.astype(bf16)
    g_proj_w = left_product(attended, middle_round)
    g_proj_b = jnp.sum(grad_middle, axis=0)
    grad_attended = right_product(middle_round, proj_mat).astype(bf16)
    scores = jnp.einsum("qhd,khd->hqk", q_heads, k_heads, preferred_element_type=f32)
    chance = jnp.exp(scores - log_total)
    again_probs = chance.astype(bf16)
    g_heads = grad_attended.reshape(local, HEADS, HEAD_DIM)
    a_heads = attended.reshape(local, HEADS, HEAD_DIM)
    grad_probs = jnp.einsum("qhd,khd->hqk", g_heads, v_heads, preferred_element_type=f32)
    offsets = jnp.einsum("qhd,qhd->hq", g_heads, a_heads, preferred_element_type=f32)[:, :, None]
    grad_scores = (chance * (grad_probs - offsets)).astype(bf16)
    grad_queries = (
        jnp.einsum("hqk,khd->qhd", grad_scores, k_heads, preferred_element_type=f32) * scale
    ).reshape(local, width)
    key_terms = jnp.einsum(
        "hqk,qhd->khd", grad_scores, q_heads, preferred_element_type=f32
    ).reshape(-1, width)
    value_terms = jnp.einsum(
        "hqk,qhd->khd", again_probs, g_heads, preferred_element_type=f32
    ).reshape(-1, width)
    pair = lax.psum_scatter(
        jnp.concatenate([key_terms, value_terms], axis=1), "frame", scatter_dimension=0, tiled=True
    )
    grad_keys, grad_values = pair[:, :width], pair[:, width:]
    query_round = grad_queries.astype(bf16)
    key_round = grad_keys.astype(bf16)
    value_round = grad_values.astype(bf16)
    g_query_w = left_product(first_hidden, query_round)
    g_key_w = left_product(first_hidden, key_round)
    g_value_w = left_product(first_hidden, value_round)
    g_query_b = jnp.sum(grad_queries, axis=0)
    g_value_b = jnp.sum(grad_values, axis=0)
    grad_first = (
        right_product(query_round, query_mat)
        + right_product(key_round, key_mat)
        + right_product(value_round, value_mat)
    )
    g_first_g = jnp.sum(grad_first * first_norm, axis=0)
    g_first_b = jnp.sum(grad_first, axis=0)
    input_grad = (
        grad_middle + norm_back(grad_first * pre_gain.astype(f32), first_norm, first_rstd)
    ).astype(bf16)
    small_grads = [
        item.reshape(-1, 1)
        for item in (
            g_first_g,
            g_first_b,
            g_query_b,
            g_value_b,
            g_proj_b,
            g_second_g,
            g_second_b,
            g_outer_b,
        )
    ]
    small_grads.append(
        g_inner_b.reshape(total // own, per, own).transpose(0, 2, 1).reshape(total, per)
    )
    small_grads = jnp.concatenate(small_grads, axis=1)
    small_grads = jnp.pad(small_grads, ((0, 0), (0, -small_grads.shape[1] % 128)))
    o_outer_w = scatter_rows(g_outer_w.astype(bf16)).astype(f32)
    last = scatter_rows(
        jnp.concatenate(
            [g_query_w, g_key_w, g_value_w, g_proj_w, g_inner_w, small_grads], axis=1
        ).astype(bf16)
    ).astype(f32)
    (o_query_w, o_key_w, o_value_w, o_proj_w, o_inner_w, o_small) = jnp.split(
        last, ends[:-1], axis=1
    )
    (
        o_first_g,
        o_first_b,
        o_query_b,
        o_value_b,
        o_proj_b,
        o_second_g,
        o_second_b,
        o_outer_b,
    ) = [o_small[:, at] for at in range(8)]
    o_inner_b = o_small[:, 8 : 8 + per].T.reshape(-1)
    return (
        layer_output,
        input_grad,
        o_first_g,
        o_first_b,
        o_query_w,
        o_query_b,
        o_key_w,
        o_value_w,
        o_value_b,
        o_proj_w,
        o_proj_b,
        o_second_g,
        o_second_b,
        o_inner_w,
        o_inner_b,
        o_outer_w,
        o_outer_b,
    )


def solution(mesh):
    placed = (
        P(("clip", "frame"), None),
        P(("clip", "frame")),
        P(("clip", "frame")),
        P(("clip", "frame"), None),
        P(("clip", "frame")),
        P(("clip", "frame"), None),
        P(("clip", "frame"), None),
        P(("clip", "frame")),
        P(("clip", "frame"), None),
        P(("clip", "frame")),
        P(("clip", "frame")),
        P(("clip", "frame")),
        P(("clip", "frame"), None),
        P(("clip", "frame")),
        P(("clip", "frame"), None),
        P(("clip", "frame")),
        P(("clip", "frame"), None),
    )
    return jax.shard_map(
        body,
        mesh=mesh,
        in_specs=placed,
        out_specs=(
            P(("clip", "frame"), None),
            P(("clip", "frame"), None),
            P(("clip", "frame")),
            P(("clip", "frame")),
            P(("clip", "frame"), None),
            P(("clip", "frame")),
            P(("clip", "frame"), None),
            P(("clip", "frame"), None),
            P(("clip", "frame")),
            P(("clip", "frame"), None),
            P(("clip", "frame")),
            P(("clip", "frame")),
            P(("clip", "frame")),
            P(("clip", "frame"), None),
            P(("clip", "frame")),
            P(("clip", "frame"), None),
            P(("clip", "frame")),
        ),
        check_vma=False,
    )
```

```python
import functools

import jax
import jax.numpy as jnp
from jax import lax
from jax.experimental import pallas as pl
from jax.experimental.pallas import tpu as pltpu
from jax.sharding import PartitionSpec as P

HEADS = 12
HEAD_DIM = 64


EPS = 1e-05
SQRT_HALF = 0.7071067811865476
INV_ROOT = 0.3989422804014327


def normalize(rows):
    mean = jnp.mean(rows, axis=-1, keepdims=True)
    centered = rows - mean
    rstd = lax.rsqrt(jnp.mean(centered * centered, axis=-1, keepdims=True) + EPS)
    return (centered * rstd, rstd)


def norm_back(grad_norm, normed, rstd):
    first = jnp.mean(grad_norm, axis=-1, keepdims=True)
    second = jnp.mean(grad_norm * normed, axis=-1, keepdims=True)
    return rstd * (grad_norm - first - normed * second)


def gelu_slope(inner):
    return (
        0.5 * (1.0 + lax.erf(inner * SQRT_HALF)) + inner * jnp.exp(-0.5 * inner * inner) * INV_ROOT
    )


def matmul(left, right):
    return jnp.dot(left, right, preferred_element_type=jnp.float32)


def left_product(left, right):
    return jnp.einsum("ti,to->io", left, right, preferred_element_type=jnp.float32)


def right_product(left, right):
    return jnp.einsum("to,io->ti", left, right, preferred_element_type=jnp.float32)


AXES = ("clip", "frame")
f32 = jnp.float32
bf16 = jnp.bfloat16


def as_columns(vectors, rows):
    return jnp.concatenate([item.reshape(-1, rows).T for item in vectors], axis=1)


def gather_rows(part):
    return lax.all_gather(part, AXES, axis=0, tiled=True)


def reversed_bits(value, bits):
    total = 0
    for at in range(bits):
        total = total + ((value // 2**at) % 2) * 2 ** (bits - 1 - at)
    return total


def halving_steps(clip, frame, clip_bits, frame_bits):
    core = clip % 2
    steps = [(core, clip + 1 - 2 * core, frame)]
    for step in range(1, clip_bits):
        down, up = 2 ** (clip_bits - step), 2**step
        bit = ((clip // down) % 2) * (1 - core) + ((clip // up) % 2) * core
        stride = down * (1 - core) + up * core
        steps.append((bit, clip + (1 - 2 * bit) * stride, frame))
    for step in range(frame_bits):
        bit = (frame // 2**step) % 2
        steps.append((bit, clip, frame + (1 - 2 * bit) * 2**step))
    return steps


def greet(steps):
    barrier = pltpu.get_barrier_semaphore()
    for _, clip, frame in steps:
        pl.semaphore_signal(
            barrier, inc=1, device_id=(clip, frame), device_id_type=pl.DeviceIdType.MESH
        )
    pl.semaphore_wait(barrier, len(steps))


def scatter_kernel(clip_bits, frame_bits, terms, out, *scratch):
    count = clip_bits + frame_bits
    current, arrived = scratch[0], scratch[1 : 1 + count]
    send_sems, recv_sems = scratch[1 + count], scratch[2 + count]
    clip, frame = lax.axis_index("clip"), lax.axis_index("frame")
    steps = halving_steps(clip, frame, clip_bits, frame_bits)
    greet(steps)
    core = steps[0][0]
    frames = 2**frame_bits

    def push(step, source):
        copy = pltpu.make_async_remote_copy(
            src_ref=source,
            dst_ref=arrived[step],
            send_sem=send_sems.at[step],
            recv_sem=recv_sems.at[step],
            device_id=(steps[step][1], steps[step][2]),
            device_id_type=pl.DeviceIdType.MESH,
        )
        copy.start()
        copy.wait()

    push(0, terms.at[:, 1 - core])

    def first_sum(at, carry):
        group, lane = at // frames, at % frames
        slot = group * (1 - core) + reversed_bits(group, clip_bits - 1) * core
        slot = slot * frames + reversed_bits(lane, frame_bits)
        current[slot] = (
            terms[group, core, lane].astype(f32) + arrived[0][group, lane].astype(f32)
        ).astype(bf16)
        return carry

    lax.fori_loop(0, current.shape[0], first_sum, 0)
    held = current
    for step in range(1, count):
        bit = steps[step][0]
        half = held.shape[0] // 2
        push(step, held.at[pl.ds((1 - bit) * half, half)])
        if step == count - 1:
            out[...] = held[bit].astype(f32) + arrived[step][0].astype(f32)
            break

        def next_sum(at, carry, held=held, step=step, bit=bit, half=half):
            arrived[step][at] = (
                held[bit * half + at].astype(f32) + arrived[step][at].astype(f32)
            ).astype(bf16)
            return carry

        lax.fori_loop(0, half, next_sum, 0)
        held = arrived[step]


def scatter_blocks(blocks, clips, frames):
    count, rows, columns = blocks.shape
    clip_bits, frame_bits = clips.bit_length() - 1, frames.bit_length() - 1
    steps = clip_bits + frame_bits
    arrivals = [pltpu.VMEM((clips // 2, frames, rows, columns), bf16)]
    for step in range(1, steps):
        arrivals.append(pltpu.VMEM((count >> (step + 1), rows, columns), bf16))
    return pl.pallas_call(
        functools.partial(scatter_kernel, clip_bits, frame_bits),
        out_shape=jax.ShapeDtypeStruct((rows, columns), f32),
        in_specs=[pl.BlockSpec(memory_space=pltpu.VMEM)],
        out_specs=pl.BlockSpec(memory_space=pltpu.VMEM),
        scratch_shapes=[pltpu.VMEM((count // 2, rows, columns), bf16)]
        + arrivals
        + [pltpu.SemaphoreType.DMA((steps,)), pltpu.SemaphoreType.DMA((steps,))],
        compiler_params=pltpu.CompilerParams(
            collective_id=1, has_side_effects=True, vmem_limit_bytes=52 * 2**20
        ),
    )(blocks.reshape(clips // 2, 2, frames, rows, columns))


def body(
    layer_input,
    first_gain,
    first_bias,
    query_weight,
    query_bias,
    key_weight,
    value_weight,
    value_bias,
    output_weight,
    output_bias,
    second_gain,
    second_bias,
    inner_weight,
    inner_bias,
    outer_weight,
    outer_bias,
    upstream,
):
    scale = HEAD_DIM ** (-0.5)
    own = query_weight.shape[0]
    vectors = (
        first_gain,
        first_bias,
        query_bias,
        value_bias,
        output_bias,
        second_gain,
        second_bias,
        outer_bias,
    )
    small = as_columns(vectors + (inner_bias,), own)
    spare = -small.shape[1] % 128
    small = jnp.pad(small, ((0, 0), (0, spare)))
    sizes = (
        query_weight.shape[1],
        key_weight.shape[1],
        value_weight.shape[1],
        output_weight.shape[1],
        inner_weight.shape[1],
        small.shape[1],
    )
    ends = []
    for size in sizes:
        ends.append((ends[-1] if ends else 0) + size)
    wide = gather_rows(
        jnp.concatenate(
            [query_weight, key_weight, value_weight, output_weight, inner_weight, small], axis=1
        )
    )
    wide, outer_weight = lax.optimization_barrier((wide, outer_weight))
    outer_mat = gather_rows(outer_weight)
    (query_mat, key_mat, value_mat, proj_mat, inner_mat, shared) = jnp.split(wide, ends[:-1], axis=1)
    total = query_mat.shape[0]
    (pre_gain, pre_shift, query_add, value_add, proj_add, post_gain, post_shift, outer_add) = [
        shared[:, at] for at in range(8)
    ]
    per = inner_bias.shape[0] // own
    inner_add = (
        shared[:, 8 : 8 + per].reshape(total // own, own, per).transpose(0, 2, 1).reshape(-1)
    )
    local = layer_input.shape[0]
    width = layer_input.shape[1]
    rows = layer_input.astype(f32)
    first_norm, first_rstd = normalize(rows)
    first_hidden = (first_norm * pre_gain.astype(f32) + pre_shift.astype(f32)).astype(bf16)
    queries = ((matmul(first_hidden, query_mat) + query_add.astype(f32)) * scale).astype(bf16)
    keys = matmul(first_hidden, key_mat).astype(bf16)
    values = (matmul(first_hidden, value_mat) + value_add.astype(f32)).astype(bf16)
    both = lax.all_gather(jnp.concatenate([keys, values], axis=1), "frame", axis=0, tiled=True)
    all_keys, all_values = both[:, :width], both[:, width:]
    q_heads = queries.reshape(local, HEADS, HEAD_DIM)
    k_heads = all_keys.reshape(-1, HEADS, HEAD_DIM)
    v_heads = all_values.reshape(-1, HEADS, HEAD_DIM)
    scores = jnp.einsum("qhd,khd->hqk", q_heads, k_heads, preferred_element_type=f32)
    log_total = jax.nn.logsumexp(scores, axis=-1, keepdims=True)
    probs = jnp.exp(scores - log_total).astype(bf16)
    attended = (
        jnp.einsum("hqk,khd->qhd", probs, v_heads, preferred_element_type=f32)
        .reshape(local, width)
        .astype(bf16)
    )
    middle = rows + matmul(attended, proj_mat) + proj_add.astype(f32)
    second_norm, second_rstd = normalize(middle)
    second_hidden = (second_norm * post_gain.astype(f32) + post_shift.astype(f32)).astype(bf16)
    inner = matmul(second_hidden, inner_mat) + inner_add.astype(f32)
    activated = jax.nn.gelu(inner, approximate=False).astype(bf16)
    layer_output = (middle + matmul(activated, outer_mat) + outer_add.astype(f32)).astype(bf16)
    grad_out = upstream.astype(f32)
    g_outer_w = left_product(activated, upstream)
    g_outer_b = jnp.sum(grad_out, axis=0)
    grad_inner = right_product(upstream, outer_mat) * gelu_slope(inner)
    inner_round = grad_inner.astype(bf16)
    g_inner_w = left_product(second_hidden, inner_round)
    g_inner_b = jnp.sum(grad_inner, axis=0)
    grad_second = right_product(inner_round, inner_mat)
    g_second_g = jnp.sum(grad_second * second_norm, axis=0)
    g_second_b = jnp.sum(grad_second, axis=0)
    grad_middle = grad_out + norm_back(
        grad_second * post_gain.astype(f32), second_norm, second_rstd
    )
    middle_round = grad_middle.astype(bf16)
    g_proj_w = left_product(attended, middle_round)
    g_proj_b = jnp.sum(grad_middle, axis=0)
    grad_attended = right_product(middle_round, proj_mat).astype(bf16)
    scores = jnp.einsum("qhd,khd->hqk", q_heads, k_heads, preferred_element_type=f32)
    chance = jnp.exp(scores - log_total)
    again_probs = chance.astype(bf16)
    g_heads = grad_attended.reshape(local, HEADS, HEAD_DIM)
    a_heads = attended.reshape(local, HEADS, HEAD_DIM)
    grad_probs = jnp.einsum("qhd,khd->hqk", g_heads, v_heads, preferred_element_type=f32)
    offsets = jnp.einsum("qhd,qhd->hq", g_heads, a_heads, preferred_element_type=f32)[:, :, None]
    grad_scores = (chance * (grad_probs - offsets)).astype(bf16)
    grad_queries = (
        jnp.einsum("hqk,khd->qhd", grad_scores, k_heads, preferred_element_type=f32) * scale
    ).reshape(local, width)
    key_terms = jnp.einsum(
        "hqk,qhd->khd", grad_scores, q_heads, preferred_element_type=f32
    ).reshape(-1, width)
    value_terms = jnp.einsum(
        "hqk,qhd->khd", again_probs, g_heads, preferred_element_type=f32
    ).reshape(-1, width)
    pair = lax.psum_scatter(
        jnp.concatenate([key_terms, value_terms], axis=1).astype(bf16), "frame", scatter_dimension=0, tiled=True
    )
    pair = pair.astype(f32)
    grad_keys, grad_values = pair[:, :width], pair[:, width:]
    query_round = grad_queries.astype(bf16)
    key_round = grad_keys.astype(bf16)
    value_round = grad_values.astype(bf16)
    g_query_w = left_product(first_hidden, query_round)
    g_key_w = left_product(first_hidden, key_round)
    g_value_w = left_product(first_hidden, value_round)
    g_query_b = jnp.sum(grad_queries, axis=0)
    g_value_b = jnp.sum(grad_values, axis=0)
    grad_first = (
        right_product(query_round, query_mat)
        + right_product(key_round, key_mat)
        + right_product(value_round, value_mat)
    )
    g_first_g = jnp.sum(grad_first * first_norm, axis=0)
    g_first_b = jnp.sum(grad_first, axis=0)
    input_grad = (
        grad_middle + norm_back(grad_first * pre_gain.astype(f32), first_norm, first_rstd)
    ).astype(bf16)
    small_grads = [
        item.reshape(-1, 1)
        for item in (
            g_first_g,
            g_first_b,
            g_query_b,
            g_value_b,
            g_proj_b,
            g_second_g,
            g_second_b,
            g_outer_b,
        )
    ]
    small_grads.append(
        g_inner_b.reshape(total // own, per, own).transpose(0, 2, 1).reshape(total, per)
    )
    devices = total // own
    small_grads = jnp.concatenate(small_grads, axis=1)
    kinds = small_grads.shape[1]
    small_rows = small_grads.reshape(devices, own, kinds).transpose(0, 2, 1).reshape(devices, -1)
    used = 4 * own + g_inner_w.shape[1] // width * own + g_outer_w.shape[0] // devices
    tail = -(-small_rows.shape[1] // width)
    tail += -(used + tail) % 16
    small_rows = jnp.pad(small_rows, ((0, 0), (0, tail * width - small_rows.shape[1])))
    pieces = [g_query_w, g_key_w, g_value_w, g_proj_w]
    pieces += [g_inner_w[:, at : at + width] for at in range(0, g_inner_w.shape[1], width)]
    pieces += [g_outer_w, small_rows.reshape(devices * tail, width)]
    blocks = jnp.concatenate(
        [item.reshape(devices, -1, width).astype(bf16) for item in pieces], axis=1
    )
    mine = scatter_blocks(blocks, lax.axis_size("clip"), lax.axis_size("frame"))
    (o_query_w, o_key_w, o_value_w, o_proj_w) = [
        mine[at * own : (at + 1) * own] for at in range(4)
    ]
    o_inner_w = jnp.concatenate(
        [mine[at * own : (at + 1) * own] for at in range(4, 4 + g_inner_w.shape[1] // width)],
        axis=1,
    )
    o_outer_w = mine[used - g_outer_w.shape[0] // devices : used]
    o_small = mine[used:].reshape(-1)[: kinds * own].reshape(kinds, own)
    (
        o_first_g,
        o_first_b,
        o_query_b,
        o_value_b,
        o_proj_b,
        o_second_g,
        o_second_b,
        o_outer_b,
    ) = [o_small[at] for at in range(8)]
    o_inner_b = o_small[8:].reshape(-1)
    return (
        layer_output,
        input_grad,
        o_first_g,
        o_first_b,
        o_query_w,
        o_query_b,
        o_key_w,
        o_value_w,
        o_value_b,
        o_proj_w,
        o_proj_b,
        o_second_g,
        o_second_b,
        o_inner_w,
        o_inner_b,
        o_outer_w,
        o_outer_b,
    )


def solution(mesh):
    placed = (
        P(("clip", "frame"), None),
        P(("clip", "frame")),
        P(("clip", "frame")),
        P(("clip", "frame"), None),
        P(("clip", "frame")),
        P(("clip", "frame"), None),
        P(("clip", "frame"), None),
        P(("clip", "frame")),
        P(("clip", "frame"), None),
        P(("clip", "frame")),
        P(("clip", "frame")),
        P(("clip", "frame")),
        P(("clip", "frame"), None),
        P(("clip", "frame")),
        P(("clip", "frame"), None),
        P(("clip", "frame")),
        P(("clip", "frame"), None),
    )
    return jax.shard_map(
        body,
        mesh=mesh,
        in_specs=placed,
        out_specs=(
            P(("clip", "frame"), None),
            P(("clip", "frame"), None),
            P(("clip", "frame")),
            P(("clip", "frame")),
            P(("clip", "frame"), None),
            P(("clip", "frame")),
            P(("clip", "frame"), None),
            P(("clip", "frame"), None),
            P(("clip", "frame")),
            P(("clip", "frame"), None),
            P(("clip", "frame")),
            P(("clip", "frame")),
            P(("clip", "frame")),
            P(("clip", "frame"), None),
            P(("clip", "frame")),
            P(("clip", "frame"), None),
            P(("clip", "frame")),
        ),
        check_vma=False,
    )
```

```python
import functools

import jax
import jax.numpy as jnp
from jax import lax
from jax.experimental import pallas as pl
from jax.experimental.pallas import tpu as pltpu
from jax.sharding import PartitionSpec as P

HEADS = 12
HEAD_DIM = 64


EPS = 1e-05
SQRT_HALF = 0.7071067811865476
INV_ROOT = 0.3989422804014327


def normalize(rows):
    mean = jnp.mean(rows, axis=-1, keepdims=True)
    centered = rows - mean
    rstd = lax.rsqrt(jnp.mean(centered * centered, axis=-1, keepdims=True) + EPS)
    return (centered * rstd, rstd)


def norm_back(grad_norm, normed, rstd):
    first = jnp.mean(grad_norm, axis=-1, keepdims=True)
    second = jnp.mean(grad_norm * normed, axis=-1, keepdims=True)
    return rstd * (grad_norm - first - normed * second)


def gelu_slope(inner):
    return (
        0.5 * (1.0 + lax.erf(inner * SQRT_HALF)) + inner * jnp.exp(-0.5 * inner * inner) * INV_ROOT
    )


def matmul(left, right):
    return jnp.dot(left, right, preferred_element_type=jnp.float32)


def left_product(left, right):
    return jnp.einsum("ti,to->io", left, right, preferred_element_type=jnp.float32)


def right_product(left, right):
    return jnp.einsum("to,io->ti", left, right, preferred_element_type=jnp.float32)


AXES = ("clip", "frame")
f32 = jnp.float32
bf16 = jnp.bfloat16


def as_columns(vectors, rows):
    return jnp.concatenate([item.reshape(-1, rows).T for item in vectors], axis=1)


def gather_rows(part):
    return lax.all_gather(part, AXES, axis=0, tiled=True)


def reversed_bits(value, bits):
    total = 0
    for at in range(bits):
        total = total + ((value // 2**at) % 2) * 2 ** (bits - 1 - at)
    return total


def halving_steps(clip, frame, clip_bits, frame_bits):
    core = clip % 2
    steps = [(core, clip + 1 - 2 * core, frame)]
    for step in range(1, clip_bits):
        down, up = 2 ** (clip_bits - step), 2**step
        bit = ((clip // down) % 2) * (1 - core) + ((clip // up) % 2) * core
        stride = down * (1 - core) + up * core
        steps.append((bit, clip + (1 - 2 * bit) * stride, frame))
    for step in range(frame_bits):
        bit = (frame // 2**step) % 2
        steps.append((bit, clip, frame + (1 - 2 * bit) * 2**step))
    return steps


def greet(steps):
    barrier = pltpu.get_barrier_semaphore()
    for _, clip, frame in steps:
        pl.semaphore_signal(
            barrier, inc=1, device_id=(clip, frame), device_id_type=pl.DeviceIdType.MESH
        )
    pl.semaphore_wait(barrier, len(steps))


def scatter_kernel(clip_bits, frame_bits, chunks, terms, out, *scratch):
    count = clip_bits + frame_bits
    current, arrived = scratch[0], scratch[1 : 1 + count]
    send_sems, recv_sems = scratch[1 + count], scratch[2 + count]
    clip, frame = lax.axis_index("clip"), lax.axis_index("frame")
    steps = halving_steps(clip, frame, clip_bits, frame_bits)
    greet(steps)
    core = steps[0][0]
    frames = 2**frame_bits

    def push(step, chunk, source):
        rows = pl.ds(*chunks[chunk])
        target = arrived[step].at[:, :, rows] if step == 0 else arrived[step].at[:, rows]
        copy = pltpu.make_async_remote_copy(
            src_ref=source,
            dst_ref=target,
            send_sem=send_sems.at[step, chunk],
            recv_sem=recv_sems.at[step, chunk],
            device_id=(steps[step][1], steps[step][2]),
            device_id_type=pl.DeviceIdType.MESH,
        )
        copy.start()
        return copy

    flying = [
        push(0, chunk, terms.at[:, 1 - core, :, pl.ds(*chunks[chunk])])
        for chunk in range(len(chunks))
    ]
    held = current
    for step in range(count):
        for chunk, (first, size) in enumerate(chunks):
            rows = pl.ds(first, size)
            flying[chunk].wait()
            if step == 0:

                def first_sum(at, carry, rows=rows):
                    group, lane = at // frames, at % frames
                    slot = group * (1 - core) + reversed_bits(group, clip_bits - 1) * core
                    slot = slot * frames + reversed_bits(lane, frame_bits)
                    current[slot, rows] = (
                        terms[group, core, lane, rows].astype(f32)
                        + arrived[0][group, lane, rows].astype(f32)
                    ).astype(bf16)
                    return carry

                lax.fori_loop(0, current.shape[0], first_sum, 0)
                after = current
            else:
                bit, half, after = steps[step][0], held.shape[0] // 2, arrived[step]
                if step == count - 1:
                    out[rows] = held[bit, rows].astype(f32) + after[0, rows].astype(f32)
                    continue

                def next_sum(at, carry, rows=rows, held=held, after=after, bit=bit, half=half):
                    after[at, rows] = (
                        held[bit * half + at, rows].astype(f32) + after[at, rows].astype(f32)
                    ).astype(bf16)
                    return carry

                lax.fori_loop(0, half, next_sum, 0)
            away = 1 - steps[step + 1][0]
            half = after.shape[0] // 2
            flying[chunk] = push(step + 1, chunk, after.at[pl.ds(away * half, half), rows])
        held = after


def scatter_blocks(blocks, clips, frames):
    count, rows, columns = blocks.shape
    clip_bits, frame_bits = clips.bit_length() - 1, frames.bit_length() - 1
    steps = clip_bits + frame_bits
    units = rows // 16
    parts = min(4, units)
    edges = [units * part // parts * 16 for part in range(parts + 1)]
    chunks = [(first, last - first) for first, last in zip(edges[:-1], edges[1:])]
    arrivals = [pltpu.VMEM((clips // 2, frames, rows, columns), bf16)]
    for step in range(1, steps):
        arrivals.append(pltpu.VMEM((count >> (step + 1), rows, columns), bf16))
    return pl.pallas_call(
        functools.partial(scatter_kernel, clip_bits, frame_bits, chunks),
        out_shape=jax.ShapeDtypeStruct((rows, columns), f32),
        in_specs=[pl.BlockSpec(memory_space=pltpu.VMEM)],
        out_specs=pl.BlockSpec(memory_space=pltpu.VMEM),
        scratch_shapes=[pltpu.VMEM((count // 2, rows, columns), bf16)]
        + arrivals
        + [pltpu.SemaphoreType.DMA((steps, parts))] * 2,
        compiler_params=pltpu.CompilerParams(
            collective_id=1, has_side_effects=True, vmem_limit_bytes=52 * 2**20
        ),
    )(blocks.reshape(clips // 2, 2, frames, rows, columns))


def body(
    layer_input,
    first_gain,
    first_bias,
    query_weight,
    query_bias,
    key_weight,
    value_weight,
    value_bias,
    output_weight,
    output_bias,
    second_gain,
    second_bias,
    inner_weight,
    inner_bias,
    outer_weight,
    outer_bias,
    upstream,
):
    scale = HEAD_DIM ** (-0.5)
    own = query_weight.shape[0]
    vectors = (
        first_gain,
        first_bias,
        query_bias,
        value_bias,
        output_bias,
        second_gain,
        second_bias,
        outer_bias,
    )
    small = as_columns(vectors + (inner_bias,), own)
    spare = -small.shape[1] % 128
    small = jnp.pad(small, ((0, 0), (0, spare)))
    sizes = (
        query_weight.shape[1],
        key_weight.shape[1],
        value_weight.shape[1],
        output_weight.shape[1],
        inner_weight.shape[1],
        small.shape[1],
    )
    ends = []
    for size in sizes:
        ends.append((ends[-1] if ends else 0) + size)
    wide = gather_rows(
        jnp.concatenate(
            [
                query_weight,
                key_weight,
                value_weight,
                output_weight,
                inner_weight,
                small,
                outer_weight.reshape(own, -1),
            ],
            axis=1,
        )
    )
    (query_mat, key_mat, value_mat, proj_mat, inner_mat, shared, outer_mat) = jnp.split(wide, ends, axis=1)
    total = query_mat.shape[0]
    outer_mat = outer_mat.reshape(-1, outer_weight.shape[1])
    (pre_gain, pre_shift, query_add, value_add, proj_add, post_gain, post_shift, outer_add) = [
        shared[:, at] for at in range(8)
    ]
    per = inner_bias.shape[0] // own
    inner_add = (
        shared[:, 8 : 8 + per].reshape(total // own, own, per).transpose(0, 2, 1).reshape(-1)
    )
    local = layer_input.shape[0]
    width = layer_input.shape[1]
    rows = layer_input.astype(f32)
    first_norm, first_rstd = normalize(rows)
    first_hidden = (first_norm * pre_gain.astype(f32) + pre_shift.astype(f32)).astype(bf16)
    queries = ((matmul(first_hidden, query_mat) + query_add.astype(f32)) * scale).astype(bf16)
    keys = matmul(first_hidden, key_mat).astype(bf16)
    values = (matmul(first_hidden, value_mat) + value_add.astype(f32)).astype(bf16)
    both = lax.all_gather(jnp.concatenate([keys, values], axis=1), "frame", axis=0, tiled=True)
    all_keys, all_values = both[:, :width], both[:, width:]
    q_heads = queries.reshape(local, HEADS, HEAD_DIM)
    k_heads = all_keys.reshape(-1, HEADS, HEAD_DIM)
    v_heads = all_values.reshape(-1, HEADS, HEAD_DIM)
    scores = jnp.einsum("qhd,khd->hqk", q_heads, k_heads, preferred_element_type=f32)
    log_total = jax.nn.logsumexp(scores, axis=-1, keepdims=True)
    probs = jnp.exp(scores - log_total).astype(bf16)
    attended = (
        jnp.einsum("hqk,khd->qhd", probs, v_heads, preferred_element_type=f32)
        .reshape(local, width)
        .astype(bf16)
    )
    middle = rows + matmul(attended, proj_mat) + proj_add.astype(f32)
    second_norm, second_rstd = normalize(middle)
    second_hidden = (second_norm * post_gain.astype(f32) + post_shift.astype(f32)).astype(bf16)
    inner = matmul(second_hidden, inner_mat) + inner_add.astype(f32)
    activated = jax.nn.gelu(inner, approximate=False).astype(bf16)
    layer_output = (middle + matmul(activated, outer_mat) + outer_add.astype(f32)).astype(bf16)
    grad_out = upstream.astype(f32)
    g_outer_w = left_product(activated, upstream)
    g_outer_b = jnp.sum(grad_out, axis=0)
    grad_inner = right_product(upstream, outer_mat) * gelu_slope(inner)
    inner_round = grad_inner.astype(bf16)
    g_inner_w = left_product(second_hidden, inner_round)
    g_inner_b = jnp.sum(grad_inner, axis=0)
    grad_second = right_product(inner_round, inner_mat)
    g_second_g = jnp.sum(grad_second * second_norm, axis=0)
    g_second_b = jnp.sum(grad_second, axis=0)
    grad_middle = grad_out + norm_back(
        grad_second * post_gain.astype(f32), second_norm, second_rstd
    )
    middle_round = grad_middle.astype(bf16)
    g_proj_w = left_product(attended, middle_round)
    g_proj_b = jnp.sum(grad_middle, axis=0)
    grad_attended = right_product(middle_round, proj_mat).astype(bf16)
    scores = jnp.einsum("qhd,khd->hqk", q_heads, k_heads, preferred_element_type=f32)
    chance = jnp.exp(scores - log_total)
    again_probs = chance.astype(bf16)
    g_heads = grad_attended.reshape(local, HEADS, HEAD_DIM)
    a_heads = attended.reshape(local, HEADS, HEAD_DIM)
    grad_probs = jnp.einsum("qhd,khd->hqk", g_heads, v_heads, preferred_element_type=f32)
    offsets = jnp.einsum("qhd,qhd->hq", g_heads, a_heads, preferred_element_type=f32)[:, :, None]
    grad_scores = (chance * (grad_probs - offsets)).astype(bf16)
    grad_queries = (
        jnp.einsum("hqk,khd->qhd", grad_scores, k_heads, preferred_element_type=f32) * scale
    ).reshape(local, width)
    key_terms = jnp.einsum(
        "hqk,qhd->khd", grad_scores, q_heads, preferred_element_type=f32
    ).reshape(-1, width)
    value_terms = jnp.einsum(
        "hqk,qhd->khd", again_probs, g_heads, preferred_element_type=f32
    ).reshape(-1, width)
    pair = lax.psum_scatter(
        jnp.concatenate([key_terms, value_terms], axis=1).astype(bf16), "frame", scatter_dimension=0, tiled=True
    )
    pair = pair.astype(f32)
    grad_keys, grad_values = pair[:, :width], pair[:, width:]
    query_round = grad_queries.astype(bf16)
    key_round = grad_keys.astype(bf16)
    value_round = grad_values.astype(bf16)
    g_query_w = left_product(first_hidden, query_round)
    g_key_w = left_product(first_hidden, key_round)
    g_value_w = left_product(first_hidden, value_round)
    g_query_b = jnp.sum(grad_queries, axis=0)
    g_value_b = jnp.sum(grad_values, axis=0)
    grad_first = (
        right_product(query_round, query_mat)
        + right_product(key_round, key_mat)
        + right_product(value_round, value_mat)
    )
    g_first_g = jnp.sum(grad_first * first_norm, axis=0)
    g_first_b = jnp.sum(grad_first, axis=0)
    input_grad = (
        grad_middle + norm_back(grad_first * pre_gain.astype(f32), first_norm, first_rstd)
    ).astype(bf16)
    small_grads = [
        item.reshape(-1, 1)
        for item in (
            g_first_g,
            g_first_b,
            g_query_b,
            g_value_b,
            g_proj_b,
            g_second_g,
            g_second_b,
            g_outer_b,
        )
    ]
    small_grads.append(
        g_inner_b.reshape(total // own, per, own).transpose(0, 2, 1).reshape(total, per)
    )
    devices = total // own
    small_grads = jnp.concatenate(small_grads, axis=1)
    kinds = small_grads.shape[1]
    small_rows = small_grads.reshape(devices, own, kinds).transpose(0, 2, 1).reshape(devices, -1)
    used = 4 * own + g_inner_w.shape[1] // width * own + g_outer_w.shape[0] // devices
    tail = -(-small_rows.shape[1] // width)
    tail += -(used + tail) % 16
    small_rows = jnp.pad(small_rows, ((0, 0), (0, tail * width - small_rows.shape[1])))
    pieces = [g_query_w, g_key_w, g_value_w, g_proj_w]
    pieces += [g_inner_w[:, at : at + width] for at in range(0, g_inner_w.shape[1], width)]
    pieces += [g_outer_w, small_rows.reshape(devices * tail, width)]
    blocks = jnp.concatenate(
        [item.reshape(devices, -1, width).astype(bf16) for item in pieces], axis=1
    )
    mine = scatter_blocks(blocks, lax.axis_size("clip"), lax.axis_size("frame"))
    (o_query_w, o_key_w, o_value_w, o_proj_w) = [
        mine[at * own : (at + 1) * own] for at in range(4)
    ]
    o_inner_w = jnp.concatenate(
        [mine[at * own : (at + 1) * own] for at in range(4, 4 + g_inner_w.shape[1] // width)],
        axis=1,
    )
    o_outer_w = mine[used - g_outer_w.shape[0] // devices : used]
    o_small = mine[used:].reshape(-1)[: kinds * own].reshape(kinds, own)
    (
        o_first_g,
        o_first_b,
        o_query_b,
        o_value_b,
        o_proj_b,
        o_second_g,
        o_second_b,
        o_outer_b,
    ) = [o_small[at] for at in range(8)]
    o_inner_b = o_small[8:].reshape(-1)
    return (
        layer_output,
        input_grad,
        o_first_g,
        o_first_b,
        o_query_w,
        o_query_b,
        o_key_w,
        o_value_w,
        o_value_b,
        o_proj_w,
        o_proj_b,
        o_second_g,
        o_second_b,
        o_inner_w,
        o_inner_b,
        o_outer_w,
        o_outer_b,
    )


def solution(mesh):
    placed = (
        P(("clip", "frame"), None),
        P(("clip", "frame")),
        P(("clip", "frame")),
        P(("clip", "frame"), None),
        P(("clip", "frame")),
        P(("clip", "frame"), None),
        P(("clip", "frame"), None),
        P(("clip", "frame")),
        P(("clip", "frame"), None),
        P(("clip", "frame")),
        P(("clip", "frame")),
        P(("clip", "frame")),
        P(("clip", "frame"), None),
        P(("clip", "frame")),
        P(("clip", "frame"), None),
        P(("clip", "frame")),
        P(("clip", "frame"), None),
    )
    return jax.shard_map(
        body,
        mesh=mesh,
        in_specs=placed,
        out_specs=(
            P(("clip", "frame"), None),
            P(("clip", "frame"), None),
            P(("clip", "frame")),
            P(("clip", "frame")),
            P(("clip", "frame"), None),
            P(("clip", "frame")),
            P(("clip", "frame"), None),
            P(("clip", "frame"), None),
            P(("clip", "frame")),
            P(("clip", "frame"), None),
            P(("clip", "frame")),
            P(("clip", "frame")),
            P(("clip", "frame")),
            P(("clip", "frame"), None),
            P(("clip", "frame")),
            P(("clip", "frame"), None),
            P(("clip", "frame")),
        ),
        check_vma=False,
    )
```
